512 devices in a mesh: stream: 8 (over x, y_hi), expert: 64 (over z, y_lo, core).
Axes of the slice: x: 4, y: 8 (y_hi: 2, y_lo: 4; y = y_hi * 4 + y_lo), z: 8, core: 2. Of those that a mesh axis runs over, the one named last changes fastest.
Arguments:
- tokens: bfloat16 [32768, 2048], P(('stream', 'expert')), may hold values from -6 to 6
- route_gates: float32 [32768, 8], P(('stream', 'expert')), may hold values from 0.1 to 1
- expert_ids: int32 [32768, 8], P(('stream', 'expert')), may hold values from 0 to 63, as said below
- slot_index: int32 [32768, 8], P(('stream', 'expert')), may hold values from -1 to 7, as said below
- gate_quant: bfloat16 [64, 2048, 1024], P('expert', None, 'stream'), may hold values from -0.125 to 0.125
- up_quant: bfloat16 [64, 2048, 1024], P('expert', None, 'stream'), may hold values from -0.125 to 0.125
- down_quant: bfloat16 [64, 2048, 1024], P('expert', None, 'stream'), may hold values from -0.1875 to 0.1875
- gate_scale: float32 [64, 16, 8], P('expert', None, 'stream'), may hold values from 0.5 to 2
- up_scale: float32 [64, 16, 8], P('expert', None, 'stream'), may hold values from 0.5 to 2
- down_scale: float32 [64, 16, 8], P('expert', None, 'stream'), may hold values from 0.5 to 2
Outputs:
- mixed: bfloat16 [32768, 2048], P(('stream', 'expert'))
The draws below stay inside these ranges and needn't reach their ends.
Inputs may be any that keep to these rules, and one draw needn't show every extreme that they name: `expert_ids`: the 8 ids of one token differ. `slot_index`: among the choices of one device's 64 tokens that name one expert, taken in token order, the first 8 get places 0, 1, ... and the rest get -1. In every draw some expert gets all 8 places from every device.
All inputs are finite; a program needn't handle non-finite values.
Results may differ from the reference program's by a relative error of at most 0.0076.
Values may be sent and summed in bfloat16 or wider, within the bound.
A program may use at most 64 MiB of HBM per device.

```python
import math
import jax
import jax.numpy as jnp
from jax import lax

D = 2048
FF = 1024
TOP = 8
QB = 128
TOK_DEV = 64
EXPERTS = 64
CAP = 8
TOKENS = 32768


def routing(key):
    block_count = TOKENS // TOK_DEV
    keys = jax.random.split(jax.random.fold_in(key, 11), 6)
    offsets = jax.random.permutation(keys[0], EXPERTS)[:TOP].astype(jnp.int32)
    first_pick = jax.random.randint(keys[1], (block_count, TOK_DEV), 0, EXPERTS)
    second_pick = jax.random.randint(keys[2], (block_count, TOK_DEV), 0, EXPERTS)
    rotation = jax.random.randint(keys[3], (), 0, EXPERTS)
    base_ids = (first_pick * second_pick // EXPERTS + rotation) % EXPERTS
    hot_expert = jax.random.randint(keys[4], (), 0, EXPERTS)
    start_at = jax.random.randint(keys[5], (block_count, 1), 0, TOK_DEV)
    in_block = (jnp.arange(TOK_DEV, dtype=jnp.int32)[None, :] - start_at) % TOK_DEV
    base_ids = jnp.where(in_block < CAP, hot_expert, base_ids)
    chosen = ((base_ids[:, :, None] + offsets[None, None, :]) % EXPERTS).astype(jnp.int32)
    one_hot = (chosen[..., None] == jnp.arange(EXPERTS, dtype=jnp.int32)).astype(jnp.int32)
    per_token = one_hot.sum(axis=2)
    earlier = jnp.cumsum(per_token, axis=1) - per_token
    places = jnp.sum(one_hot * earlier[:, :, None, :], axis=3)
    places = jnp.where(places < CAP, places, -1).astype(jnp.int32)
    return (chosen.reshape(TOKENS, TOP), places.reshape(TOKENS, TOP))


def draw_expert_ids(key, part):
    chosen, places = routing(key)
    return chosen


def draw_slot_index(key, part):
    chosen, places = routing(key)
    return places


def steps_of(key, extent, cuts, low, top_value):
    def one(dim, shards_of):
        steps = jax.random.uniform(jax.random.fold_in(jax.random.fold_in(key, 6), dim), (shards_of,), jnp.float32, low / len(cuts), top_value / len(cuts))
        return jnp.repeat(jnp.exp(steps), extent[dim] // shards_of).reshape((-1,) + (1,) * (len(extent) - dim - 1))

    factor_of = one(*cuts[0])
    for cut in cuts[1:]:
        factor_of = factor_of * one(*cut)
    return factor_of


def bell_draw(rng, extent, width, limit, shards=(), held_as=jnp.bfloat16):
    drawn = width * jax.random.normal(rng, extent, jnp.float32)
    if shards:
        drawn = drawn * steps_of(rng, extent, shards, -0.22, 0.18)
    return jnp.clip(drawn, -limit, limit).astype(held_as)


def setup_inputs(seed: int = 0) -> dict:
    arg_keys = jax.random.split(jax.random.key(seed), 11)
    return {
        "tokens": bell_draw(arg_keys[0], (TOKENS, D), 1.0, 6.0, ((0, 512),)),
        "route_gates": jnp.clip(jnp.exp(math.log(1.0) - 2.3025851 * jax.random.uniform(arg_keys[1], (TOKENS, TOP), jnp.float32) ** steps_of(arg_keys[1], (TOKENS, TOP), ((0, 512),), -0.2, 0.2)), 0.1, 1.0),
        "expert_ids": draw_expert_ids(jax.random.fold_in(arg_keys[10], 71), 0),
        "slot_index": draw_slot_index(jax.random.fold_in(arg_keys[10], 71), 0),
        "gate_quant": bell_draw(arg_keys[4], (EXPERTS, D, FF), D ** -0.5, 0.125, ((0, 64), (2, 8))),
        "up_quant": bell_draw(arg_keys[5], (EXPERTS, D, FF), D ** -0.5, 0.125, ((0, 64), (2, 8))),
        "down_quant": bell_draw(arg_keys[6], (EXPERTS, D, FF), FF ** -0.5, 0.1875, ((0, 64), (2, 8))),
        "gate_scale": jnp.clip(jnp.exp(math.log(2.0) - 1.3862944 * jax.random.uniform(arg_keys[7], (EXPERTS, D // QB, FF // QB), jnp.float32) ** steps_of(arg_keys[7], (EXPERTS, D // QB, FF // QB), ((0, 64), (2, 8)), -0.2, 0.2)), 0.5, 2.0),
        "up_scale": jnp.clip(jnp.exp(math.log(2.0) - 1.3862944 * jax.random.uniform(arg_keys[8], (EXPERTS, D // QB, FF // QB), jnp.float32) ** steps_of(arg_keys[8], (EXPERTS, D // QB, FF // QB), ((0, 64), (2, 8)), -0.2, 0.2)), 0.5, 2.0),
        "down_scale": jnp.clip(jnp.exp(math.log(2.0) - 1.3862944 * jax.random.uniform(arg_keys[9], (EXPERTS, D // QB, FF // QB), jnp.float32) ** steps_of(arg_keys[9], (EXPERTS, D // QB, FF // QB), ((0, 64), (2, 8)), -0.2, 0.2)), 0.5, 2.0),
    }


def dequantize(quant, scales):
    expanded = jnp.repeat(jnp.repeat(scales, QB, axis=0), QB, axis=1)
    return (quant.astype(jnp.float32) * expanded).astype(jnp.bfloat16)


def reference(tokens, route_gates, expert_ids, slot_index, gate_quant, up_quant, down_quant, gate_scale, up_scale, down_scale):
    source_count = TOKENS // TOK_DEV
    token_ids = jnp.arange(TOKENS, dtype=jnp.int32)
    is_kept = slot_index >= 0
    source_dev = token_ids // TOK_DEV
    dump_slot = EXPERTS * source_count * CAP
    position = (expert_ids * source_count + source_dev[:, None]) * CAP + jnp.where(is_kept, slot_index, 0)
    position = jnp.where(is_kept, position, dump_slot).astype(jnp.int32).reshape(-1)
    owners = jnp.broadcast_to(token_ids[:, None], slot_index.shape).reshape(-1)
    row_table = jnp.full((dump_slot + 1,), TOKENS, jnp.int32).at[position].set(owners)
    row_table = jnp.where(jnp.arange(dump_slot + 1) == dump_slot, TOKENS, row_table)
    weight_table = jnp.zeros((dump_slot + 1,), jnp.float32).at[position].set(
        jnp.where(is_kept, route_gates, jnp.float32(0.0)).reshape(-1))
    row_table = row_table[:dump_slot].reshape(EXPERTS, source_count * CAP)
    weight_table = weight_table[:dump_slot].reshape(EXPERTS, source_count * CAP)
    padded = jnp.concatenate([tokens, jnp.zeros((1, D), tokens.dtype)], axis=0)

    def expert_step(running, packed):
        row_ids, weighting, gate_q, up_q, down_q, gate_s, up_s, down_s = packed
        gathered_rows = padded[row_ids]
        w_gate = dequantize(gate_q, gate_s)
        w_up = dequantize(up_q, up_s)
        w_down = dequantize(down_q, down_s)
        gate_act = jnp.dot(gathered_rows, w_gate, preferred_element_type=jnp.float32)
        up_act = jnp.dot(gathered_rows, w_up, preferred_element_type=jnp.float32)
        hidden = (jax.nn.silu(gate_act) * up_act).astype(jnp.bfloat16)
        answer = jnp.dot(hidden, w_down.T, preferred_element_type=jnp.float32).astype(jnp.bfloat16)
        running = running.at[row_ids].add(weighting[:, None] * answer.astype(jnp.float32))
        return running, None

    initial = jnp.zeros((TOKENS + 1, D), jnp.float32)
    running, _ = lax.scan(expert_step, initial, (row_table, weight_table, gate_quant, up_quant, down_quant, gate_scale, up_scale, down_scale))
    return running[:TOKENS].astype(jnp.bfloat16)
```

```python
import functools

import jax
import jax.numpy as jnp
from jax import lax
from jax.experimental import pallas as pl
from jax.experimental.pallas import tpu as pltpu
from jax.sharding import PartitionSpec as P

MESH = pl.DeviceIdType.MESH
F32 = jnp.float32
BF16 = jnp.bfloat16
GU_CHUNKS = 4
DN_CHUNKS = 2
CHUNKS = GU_CHUNKS + DN_CHUNKS
OFFSETS = (0, -1, 1, -2, 2, -3, 3, 4)
UP = (0, 1, 3, 5, 7)
DOWN = (0, 2, 4, 6, 7)


def kernel(
    tok, meta, sg, su, sd, gq, uq, dq, o_ref,
    tk, mt, ob, ib, gu, dn, lg, ld, hid, ans, ret, wh, wl, pt, rs_out, rs_in,
    w_send, w_recv, t_send, t_recv, m_send, m_recv, a_send, a_recv, b_send, b_recv, r_send, r_recv,
):
    stream, expert = lax.axis_index("stream"), lax.axis_index("expert")
    x, y_hi = stream // 2, stream % 2
    z, y_lo, core = expert // 8, (expert % 8) // 2, expert % 2
    y = 4 * y_hi + y_lo

    def dev(dx=0, dy=0, dz=0, dc=0):
        xx, yy, zz, cc = (x + dx + 4) % 4, (y + dy + 8) % 8, (z + dz + 8) % 8, (core + dc) % 2
        return (2 * xx + yy // 4, 8 * zz + 2 * (yy % 4) + cc)

    def rdma(src, dst, send, recv, device):
        return pltpu.make_async_remote_copy(
            src_ref=src, dst_ref=dst, send_sem=send, recv_sem=recv, device_id=device, device_id_type=MESH
        )

    swaps = core != y_hi
    barrier = pltpu.get_barrier_semaphore()
    peers = [dev(dx=1), dev(dx=-1), dev(dc=1), dev(dy=4, dc=1), dev(dy=1), dev(dy=-1)] + [dev(dz=k) for k in range(1, 8)]
    for peer in peers:
        pl.semaphore_signal(barrier, inc=1, device_id=peer, device_id_type=MESH)

    def dequantize(put_gu, put_dn):
        def block(b, carry):
            rows = pl.ds(pl.multiple_of(b * 128, 128), 128)
            put_gu(rows, 0, (gq[rows, :].astype(F32) * sg[b]).astype(BF16))
            put_gu(rows, 128, (uq[rows, :].astype(F32) * su[b]).astype(BF16))
            put_dn(rows, (dq[rows, :].astype(F32) * sd[b]).astype(BF16))
            return carry

        lax.fori_loop(0, 16, block, 0)

    @pl.when(swaps)
    def _():
        def put_gu(rows, lane, v):
            lg[rows, lane : lane + 128] = v

        def put_dn(rows, v):
            ld[rows, :] = v

        dequantize(put_gu, put_dn)

    @pl.when(jnp.logical_not(swaps))
    def _():
        def put_gu(rows, lane, v):
            gu[0, rows, lane : lane + 128] = v

        def put_dn(rows, v):
            dn[rows, 0:128] = v

        dequantize(put_gu, put_dn)

    tk[0] = tok[...]
    mt[0] = meta[...]
    pl.semaphore_wait(barrier, len(peers))

    def piece(slot, i, part=None):
        if i < GU_CHUNKS:
            rows = 2048 // GU_CHUNKS
            first = i * rows
        else:
            rows = 2048 // DN_CHUNKS
            first = (i - GU_CHUNKS) * rows
        if part is not None:
            rows //= 2
            first += part * rows
        if i < GU_CHUNKS:
            return gu.at[slot, pl.ds(first, rows), :]
        return dn.at[pl.ds(first, rows), pl.ds(slot * 128, 128)]

    def local_piece(i):
        if i < GU_CHUNKS:
            rows = 2048 // GU_CHUNKS
            return lg.at[pl.ds(i * rows, rows), :]
        rows = 2048 // DN_CHUNKS
        return ld.at[pl.ds((i - GU_CHUNKS) * rows, rows), :]

    def swap(i):
        return rdma(local_piece(i), piece(0, i), w_send.at[i, 0], w_recv.at[i, 0], dev(dy=4, dc=1))

    def own_up(i):
        return rdma(piece(0, i), piece(6, i), w_send.at[i, 1], w_recv.at[i, 1], dev(dx=1))

    def own_down(i):
        return rdma(piece(0, i), piece(2, i), w_send.at[i, 2], w_recv.at[i, 2], dev(dx=-1))

    def on_up(i):
        return rdma(piece(6, i, 0), piece(4, i, 0), w_send.at[i, 3], w_recv.at[i, 3], dev(dx=1))

    def on_down(i):
        return rdma(piece(2, i, 1), piece(4, i, 1), w_send.at[i, 4], w_recv.at[i, 4], dev(dx=-1))

    def share(i, r):
        return rdma(piece(2 * r, i), piece(2 * r + 1, i), w_send.at[i, 5 + r], w_recv.at[i, 5 + r], dev(dc=1))

    def tok_up(s):
        src, dst = tk.at[UP[s]], tk.at[UP[s + 1]]
        if s == 3:
            src, dst = src.at[pl.ds(0, 32), :], dst.at[pl.ds(0, 32), :]
        return rdma(src, dst, t_send.at[0, s], t_recv.at[0, s], dev(dy=1))

    def tok_down(s):
        src, dst = tk.at[DOWN[s]], tk.at[DOWN[s + 1]]
        if s == 3:
            src, dst = src.at[pl.ds(32, 32), :], dst.at[pl.ds(32, 32), :]
        return rdma(src, dst, t_send.at[1, s], t_recv.at[1, s], dev(dy=-1))

    def meta_up(s):
        return rdma(mt.at[UP[s]], mt.at[UP[s + 1]], m_send.at[0, s], m_recv.at[0, s], dev(dy=1))

    def meta_down(s):
        return rdma(mt.at[DOWN[s]], mt.at[DOWN[s + 1]], m_send.at[1, s], m_recv.at[1, s], dev(dy=-1))

    def token_start(s):
        tok_up(s).start()
        tok_down(s).start()
        meta_up(s).start()
        if s < 3:
            meta_down(s).start()

    def token_arrived(s):
        tok_up(s).wait_recv()
        tok_down(s).wait_recv()
        meta_up(s).wait_recv()
        if s < 3:
            meta_down(s).wait_recv()

    def there(p, k):
        rows = pl.ds(p * 128 + k * 16, 16)
        return rdma(ob.at[rows, :], ib.at[rows, :], a_send.at[p, k], a_recv.at[p, k], dev(dz=k))

    def back(p, k):
        rows = pl.ds(p * 128 + k * 16, 16)
        return rdma(ans.at[rows, :], ret.at[rows, :], b_send.at[p, k], b_recv.at[p, k], dev(dz=-k))

    def dispatch(p):
        row = lax.broadcasted_iota(jnp.int32, (128, 128), 0)
        lane = lax.broadcasted_iota(jnp.int32, (128, 128), 1)
        target = y * 64 + ((z + row // 16) % 8) * 8 + row % 8
        target = jnp.where((row % 16) // 8 == lane // 64, target, -5).astype(F32)
        half = lax.broadcasted_iota(jnp.int32, (16, 128), 1) // 64
        info = jnp.where(half == 0, mt[2 * p], mt[2 * p + 1])
        hit = jnp.zeros((128, 128), F32)
        weight = jnp.zeros((128, 128), F32)
        for k in range(8):
            same = target == info[k : k + 1, :]
            hit = jnp.where(same, 1.0, hit)
            weight = jnp.where(same, info[8 + k : 9 + k, :], weight)
        weight = weight.T
        high = weight.astype(BF16)
        wh[p] = high
        wl[p] = (weight - high.astype(F32)).astype(BF16)
        hit = hit.astype(BF16)
        for c in range(4):
            cols = pl.ds(c * 512, 512)
            both = jnp.concatenate([tk[2 * p, :, cols], tk[2 * p + 1, :, cols]], axis=0)
            ob[pl.ds(p * 128, 128), cols] = jnp.dot(hit, both, preferred_element_type=F32).astype(BF16)
        for k in range(1, 8):
            there(p, k).start()
        ib[pl.ds(p * 128, 16), :] = ob[pl.ds(p * 128, 16), :]

    token_start(0)

    @pl.when(swaps)
    def _():
        for i in range(CHUNKS):
            swap(i).start()

    @pl.when(jnp.logical_not(swaps))
    def _():
        for i in range(CHUNKS):
            own_up(i).start()
            own_down(i).start()
            share(i, 0).start()

    def own_round(i):
        @pl.when(swaps)
        def _():
            swap(i).wait_recv()
            own_up(i).start()
            own_down(i).start()
            share(i, 0).start()

    def forward_round(i):
        own_up(i).wait_recv()
        on_up(i).start()
        share(i, 3).start()
        own_down(i).wait_recv()
        on_down(i).start()
        share(i, 1).start()

    def far_round(i):
        on_up(i).wait_recv()
        on_down(i).wait_recv()
        share(i, 2).start()

    token_arrived(0)
    token_start(1)
    dispatch(0)
    own_round(0)
    forward_round(0)
    token_arrived(1)
    token_start(2)
    dispatch(1)
    own_round(1)
    forward_round(1)
    far_round(0)
    token_arrived(2)
    token_start(3)
    dispatch(2)
    own_round(2)
    forward_round(2)
    far_round(1)
    own_round(3)
    forward_round(3)
    far_round(2)
    token_arrived(3)
    dispatch(3)
    own_round(4)
    forward_round(4)
    far_round(3)
    own_round(5)
    forward_round(5)
    far_round(4)
    for i in range(GU_CHUNKS):
        for r in range(4):
            share(i, r).wait_recv()
    for p in range(4):
        for k in range(1, 8):
            there(p, k).wait_recv()
    far_round(5)

    def hidden_step(s, carry):
        for m in range(2):
            rows = pl.ds(m * 256, 256)
            both = jnp.dot(ib[rows, :], gu[s], preferred_element_type=F32)
            g, u = both[:, :128], both[:, 128:]
            h = g / (1.0 + jnp.exp(-g)) * u
            hid[rows, pl.ds(pl.multiple_of(s * 128, 128), 128)] = h.astype(BF16)
        return carry

    lax.fori_loop(0, 8, hidden_step, 0)
    for i in range(GU_CHUNKS, CHUNKS):
        for r in range(4):
            share(i, r).wait_recv()

    for p in (3, 2, 1, 0):
        rows = pl.ds(p * 128, 128)

        def answer_step(c, carry, rows=rows):
            cols = pl.ds(pl.multiple_of(c * 256, 256), 256)
            a = lax.dot_general(hid[rows, :], dn[cols, :], (((1,), (1,)), ((), ())), preferred_element_type=F32)
            ans[rows, cols] = a.astype(BF16)
            return carry

        lax.fori_loop(0, 8, answer_step, 0)
        for k in (4, 3, 5, 2, 6, 1, 7):
            back(p, k).start()
        ret[pl.ds(p * 128, 16), :] = ans[pl.ds(p * 128, 16), :]

    def sum_up(s):
        rows = pl.ds(0, 32 if s == 0 else 64)
        return rdma(rs_out.at[0, s, rows, :], rs_in.at[0, s, rows, :], r_send.at[0, s], r_recv.at[0, s], dev(dy=1))

    def sum_down(s):
        rows = pl.ds(32, 32) if s == 0 else pl.ds(0, 64)
        return rdma(rs_out.at[1, s, rows, :], rs_in.at[1, s, rows, :], r_send.at[1, s], r_recv.at[1, s], dev(dy=-1))

    def combine(p):
        for k in range(1, 8):
            back(p, k).wait_recv()
        for c in range(4):
            cols = pl.ds(c * 512, 512)
            r = ret[pl.ds(p * 128, 128), cols]
            pt[:, cols] = jnp.dot(wh[p], r, preferred_element_type=F32) + jnp.dot(wl[p], r, preferred_element_type=F32)

    def add_up(s, first):
        sum_up(s - 1).wait_recv()
        if s == 1:
            rs_out[0, s, 0:32, :] = (pt[first : first + 32, :] + rs_in[0, 0, 0:32, :].astype(F32)).astype(BF16)
            rs_out[0, s, 32:64, :] = pt[first + 32 : first + 64, :].astype(BF16)
        else:
            rs_out[0, s] = (pt[first : first + 64, :] + rs_in[0, s - 1].astype(F32)).astype(BF16)
        sum_up(s).start()

    def add_down(s, first):
        sum_down(s - 1).wait_recv()
        if s == 1:
            rs_out[1, s, 0:32, :] = pt[first : first + 32, :].astype(BF16)
            rs_out[1, s, 32:64, :] = (pt[first + 32 : first + 64, :] + rs_in[1, 0, 32:64, :].astype(F32)).astype(BF16)
        else:
            rs_out[1, s] = (pt[first : first + 64, :] + rs_in[1, s - 1].astype(F32)).astype(BF16)
        sum_down(s).start()

    combine(3)
    rs_out[0, 0, 0:32, :] = pt[64:96, :].astype(BF16)
    rs_out[1, 0, 32:64, :] = pt[96:128, :].astype(BF16)
    sum_up(0).start()
    sum_down(0).start()
    add_up(1, 0)
    combine(2)
    add_up(2, 0)
    add_down(1, 64)
    combine(1)
    add_up(3, 0)
    add_down(2, 64)
    combine(0)
    add_down(3, 64)
    sum_up(3).wait_recv()
    sum_down(3).wait_recv()
    o_ref[...] = (pt[0:64, :] + rs_in[0, 3].astype(F32) + rs_in[1, 3].astype(F32)).astype(BF16)

    @pl.when(swaps)
    def _():
        for i in range(CHUNKS):
            swap(i).wait_send()

    for i in range(CHUNKS):
        own_up(i).wait_send()
        own_down(i).wait_send()
        on_up(i).wait_send()
        on_down(i).wait_send()
        for r in range(4):
            share(i, r).wait_send()
    for s in range(4):
        tok_up(s).wait_send()
        tok_down(s).wait_send()
        meta_up(s).wait_send()
        if s < 3:
            meta_down(s).wait_send()
        sum_up(s).wait_send()
        sum_down(s).wait_send()
    for p in range(4):
        for k in range(1, 8):
            there(p, k).wait_send()
            back(p, k).wait_send()


def local(
    tokens,
    route_gates,
    expert_ids,
    slot_index,
    gate_quant,
    up_quant,
    down_quant,
    gate_scale,
    up_scale,
    down_scale,
):
    y_of = (expert_ids % 2) * 4 + (expert_ids // 2) % 4
    code = jnp.where(slot_index >= 0, y_of * 64 + (expert_ids // 8) * 8 + slot_index, -1).astype(F32)
    info = jnp.concatenate([code, route_gates], axis=1).T
    info = jnp.concatenate([info, info], axis=1)
    vmem = pl.BlockSpec(memory_space=pltpu.VMEM)
    smem = pl.BlockSpec(memory_space=pltpu.SMEM)
    dma = pltpu.SemaphoreType.DMA
    return pl.pallas_call(
        kernel,
        out_shape=jax.ShapeDtypeStruct((64, 2048), BF16),
        in_specs=[vmem, vmem, smem, smem, smem, vmem, vmem, vmem],
        out_specs=vmem,
        scratch_shapes=[
            pltpu.VMEM((8, 64, 2048), BF16),
            pltpu.VMEM((8, 16, 128), F32),
            pltpu.VMEM((512, 2048), BF16),
            pltpu.VMEM((512, 2048), BF16),
            pltpu.VMEM((8, 2048, 256), BF16),
            pltpu.VMEM((2048, 1024), BF16),
            pltpu.VMEM((2048, 256), BF16),
            pltpu.VMEM((2048, 128), BF16),
            pltpu.VMEM((512, 1024), BF16),
            pltpu.VMEM((512, 2048), BF16),
            pltpu.VMEM((512, 2048), BF16),
            pltpu.VMEM((4, 128, 128), BF16),
            pltpu.VMEM((4, 128, 128), BF16),
            pltpu.VMEM((128, 2048), F32),
            pltpu.VMEM((2, 4, 64, 2048), BF16),
            pltpu.VMEM((2, 4, 64, 2048), BF16),
            dma((CHUNKS, 9)),
            dma((CHUNKS, 9)),
            dma((2, 4)),
            dma((2, 4)),
            dma((2, 4)),
            dma((2, 4)),
            dma((4, 8)),
            dma((4, 8)),
            dma((4, 8)),
            dma((4, 8)),
            dma((2, 4)),
            dma((2, 4)),
        ],
        compiler_params=pltpu.CompilerParams(
            collective_id=0, has_side_effects=True, vmem_limit_bytes=56 * 2**20
        ),
        name="experts",
    )(
        tokens,
        info,
        gate_scale.reshape(16),
        up_scale.reshape(16),
        down_scale.reshape(16),
        gate_quant[0],
        up_quant[0],
        down_quant[0],
    )


def solution(mesh):
    return jax.shard_map(
        local,
        mesh=mesh,
        in_specs=(
            P(("stream", "expert"), None),
            P(("stream", "expert"), None),
            P(("stream", "expert"), None),
            P(("stream", "expert"), None),
            P("expert", None, "stream"),
            P("expert", None, "stream"),
            P("expert", None, "stream"),
            P("expert", None, "stream"),
            P("expert", None, "stream"),
            P("expert", None, "stream"),
        ),
        out_specs=P(("stream", "expert"), None),
        check_vma=False,
    )
```

```python
import functools

import jax
import jax.numpy as jnp
from jax import lax
from jax.experimental import pallas as pl
from jax.experimental.pallas import tpu as pltpu
from jax.sharding import PartitionSpec as P

MESH = pl.DeviceIdType.MESH
F32 = jnp.float32
BF16 = jnp.bfloat16
GU_CHUNKS = 4
DN_CHUNKS = 2
CHUNKS = GU_CHUNKS + DN_CHUNKS
TOKEN_TIMES = (8.0, 17.0, 25.0, 32.0)
A_FIRST, A_STEP, A_FAR = 6.0, 4.0, 5.0
SWAP_WINDOW = 2
OWN_WINDOW = 2
B_FIRST, B_STEP, B_NEXT, B_FAR = 9.0, 7.0, 7.5, 7.0
Z_ORDER = (7, 6, 5, 4, 3, 2, 1)
OFFSETS = (0, -1, 1, -2, 2, -3, 3, 4)
UP = (0, 1, 3, 5, 7)
DOWN = (0, 2, 4, 6, 7)


def kernel(
    tok, meta, sg, su, sd, gq, uq, dq, o_ref,
    tk, mt, mz, ob, ib, gu, dn, lg, ld, hid, lhs, ans, ret, wh, wl, pt, rs_out, rs_in,
    w_send, w_recv, t_send, t_recv, m_send, m_recv, n_send, n_recv, a_send, a_recv, b_send, b_recv, r_send, r_recv,
):
    stream, expert = lax.axis_index("stream"), lax.axis_index("expert")
    x, y_hi = stream // 2, stream % 2
    z, y_lo, core = expert // 8, (expert % 8) // 2, expert % 2
    y = 4 * y_hi + y_lo

    def dev(dx=0, dy=0, dz=0, dc=0):
        xx, yy, zz, cc = (x + dx + 4) % 4, (y + dy + 8) % 8, (z + dz + 8) % 8, (core + dc) % 2
        return (2 * xx + yy // 4, 8 * zz + 2 * (yy % 4) + cc)

    def rdma(src, dst, send, recv, device):
        return pltpu.make_async_remote_copy(
            src_ref=src, dst_ref=dst, send_sem=send, recv_sem=recv, device_id=device, device_id_type=MESH
        )

    swaps = core != y_hi
    barrier = pltpu.get_barrier_semaphore()
    peers = [dev(dx=1), dev(dx=-1), dev(dc=1), dev(dy=4, dc=1)]
    peers += [dev(dy=k) for k in range(1, 8)] + [dev(dz=k) for k in range(1, 8)]
    for peer in peers:
        pl.semaphore_signal(barrier, inc=1, device_id=peer, device_id_type=MESH)

    def dequantize(i):
        if i < GU_CHUNKS:
            n, first = 16 // GU_CHUNKS, i * (16 // GU_CHUNKS)
        else:
            n, first = 16 // DN_CHUNKS, (i - GU_CHUNKS) * (16 // DN_CHUNKS)

        def fill(gu_ref, dn_ref):
            def block(b, carry):
                rows = pl.ds(pl.multiple_of(b * 128, 128), 128)
                if i < GU_CHUNKS:
                    gu_ref[rows, 0:128] = (gq[rows, :].astype(F32) * sg[b]).astype(BF16)
                    gu_ref[rows, 128:256] = (uq[rows, :].astype(F32) * su[b]).astype(BF16)
                else:
                    dn_ref[rows, :] = (dq[rows, :].astype(F32) * sd[b]).astype(BF16)
                return carry

            lax.fori_loop(first, first + n, block, 0)

        pl.when(swaps)(lambda: fill(lg, ld))
        pl.when(jnp.logical_not(swaps))(lambda: fill(gu.at[0], dn.at[0]))

    tk[0] = tok[...]
    mt[0] = meta[...]
    mz[0] = meta[...]
    for i in range(CHUNKS):
        dequantize(i)
    pl.semaphore_wait(barrier, len(peers))

    def piece(slot, i, part=None):
        if i < GU_CHUNKS:
            rows = 2048 // GU_CHUNKS
            first = i * rows
        else:
            rows = 2048 // DN_CHUNKS
            first = (i - GU_CHUNKS) * rows
        if part is not None:
            rows //= 2
            first += part * rows
        if i < GU_CHUNKS:
            return gu.at[slot, pl.ds(first, rows), :]
        return dn.at[slot, pl.ds(first, rows), :]

    def local_piece(i):
        if i < GU_CHUNKS:
            rows = 2048 // GU_CHUNKS
            return lg.at[pl.ds(i * rows, rows), :]
        rows = 2048 // DN_CHUNKS
        return ld.at[pl.ds((i - GU_CHUNKS) * rows, rows), :]

    def swap(i):
        return rdma(local_piece(i), piece(0, i), w_send.at[i, 0], w_recv.at[i, 0], dev(dy=4, dc=1))

    def own_up(i):
        return rdma(piece(0, i), piece(6, i), w_send.at[i, 1], w_recv.at[i, 1], dev(dx=1))

    def own_down(i):
        return rdma(piece(0, i), piece(2, i), w_send.at[i, 2], w_recv.at[i, 2], dev(dx=-1))

    def on_up(i):
        return rdma(piece(6, i, 0), piece(4, i, 0), w_send.at[i, 3], w_recv.at[i, 3], dev(dx=1))

    def on_down(i):
        return rdma(piece(2, i, 1), piece(4, i, 1), w_send.at[i, 4], w_recv.at[i, 4], dev(dx=-1))

    def share(i, r):
        return rdma(piece(2 * r, i), piece(2 * r + 1, i), w_send.at[i, 5 + r], w_recv.at[i, 5 + r], dev(dc=1))

    def tok_up(s):
        src, dst = tk.at[UP[s]], tk.at[UP[s + 1]]
        if s == 3:
            src, dst = src.at[pl.ds(0, 32), :], dst.at[pl.ds(0, 32), :]
        return rdma(src, dst, t_send.at[0, s], t_recv.at[0, s], dev(dy=1))

    def tok_down(s):
        src, dst = tk.at[DOWN[s]], tk.at[DOWN[s + 1]]
        if s == 3:
            src, dst = src.at[pl.ds(32, 32), :], dst.at[pl.ds(32, 32), :]
        return rdma(src, dst, t_send.at[1, s], t_recv.at[1, s], dev(dy=-1))

    def meta_up(s):
        return rdma(mt.at[UP[s]], mt.at[UP[s + 1]], m_send.at[0, s], m_recv.at[0, s], dev(dy=1))

    def meta_down(s):
        return rdma(mt.at[DOWN[s]], mt.at[DOWN[s + 1]], m_send.at[1, s], m_recv.at[1, s], dev(dy=-1))

    def token_start(s):
        tok_up(s).start()
        tok_down(s).start()
        meta_up(s).start()
        if s < 3:
            meta_down(s).start()

    def token_arrived(s):
        tok_up(s).wait_recv()
        tok_down(s).wait_recv()
        meta_up(s).wait_recv()
        if s < 3:
            meta_down(s).wait_recv()

    def meta_z(k):
        return rdma(mt.at[0], mz.at[k], n_send.at[k], n_recv.at[k], dev(dz=-OFFSETS[k]))

    def there(p, k):
        rows = pl.ds(p * 128 + k * 16, 16)
        return rdma(ob.at[rows, :], ib.at[rows, :], a_send.at[p, k], a_recv.at[p, k], dev(dz=-OFFSETS[k]))

    def back(h, p, k):
        rows = pl.ds(p * 128 + k * 16, 16)
        to = dev(dz=OFFSETS[k]) if h == 0 else dev(dy=OFFSETS[k])
        return rdma(ans.at[h, rows, :], ret.at[h, rows, :], b_send.at[h, p, k], b_recv.at[h, p, k], to)

    def weigh(h, p):
        gathered = mt if h == 0 else mz
        row = lax.broadcasted_iota(jnp.int32, (128, 128), 0)
        lane = lax.broadcasted_iota(jnp.int32, (128, 128), 1)
        block = row // 16
        off = jnp.where(block % 2 == 1, -((block + 1) // 2), block // 2)
        if h == 0:
            target = y * 64 + ((z - off + 8) % 8) * 8 + row % 8
        else:
            target = ((y - off + 8) % 8) * 64 + z * 8 + row % 8
        target = jnp.where((row % 16) // 8 == lane // 64, target, -5).astype(F32)
        half = lax.broadcasted_iota(jnp.int32, (16, 128), 1) // 64
        info = jnp.where(half == 0, gathered[2 * p], gathered[2 * p + 1])
        hit = jnp.zeros((128, 128), F32)
        weight = jnp.zeros((128, 128), F32)
        for k in range(8):
            same = target == info[k : k + 1, :]
            hit = jnp.where(same, 1.0, hit)
            weight = jnp.where(same, info[8 + k : 9 + k, :], weight)
        weight = weight.T
        high = weight.astype(BF16)
        wh[h, p] = high
        wl[h, p] = (weight - high.astype(F32)).astype(BF16)
        return hit.astype(BF16)

    def dispatch(p):
        hit = weigh(0, p)
        for c in range(4):
            cols = pl.ds(c * 512, 512)
            both = jnp.concatenate([tk[2 * p, :, cols], tk[2 * p + 1, :, cols]], axis=0)
            ob[pl.ds(p * 128, 128), cols] = jnp.dot(hit, both, preferred_element_type=F32).astype(BF16)
        for k in Z_ORDER:
            there(p, k).start()
        ib[pl.ds(p * 128, 16), :] = ob[pl.ds(p * 128, 16), :]

    def own_start(i):
        own_up(i).start()
        own_down(i).start()
        share(i, 0).start()

    token_start(0)
    for k in range(1, 8):
        meta_z(k).start()

    @pl.when(swaps)
    def _():
        for i in range(SWAP_WINDOW):
            swap(i).start()

    @pl.when(jnp.logical_not(swaps))
    def _():
        for i in range(OWN_WINDOW):
            own_start(i)

    def own_round(i):
        swap(i).wait_recv()
        if i + SWAP_WINDOW < CHUNKS:
            swap(i + SWAP_WINDOW).start()
        own_start(i)

    def forward_round(i, more=False):
        own_up(i).wait_recv()
        on_up(i).start()
        own_down(i).wait_recv()
        on_down(i).start()
        if more and i + OWN_WINDOW < CHUNKS:
            own_start(i + OWN_WINDOW)
        share(i, 3).start()
        share(i, 1).start()

    def far_round(i):
        on_up(i).wait_recv()
        on_down(i).wait_recv()
        share(i, 2).start()

    def token_round(s):
        token_arrived(s)
        if s < 3:
            token_start(s + 1)
        dispatch(s)

    def run(events):
        def some():
            for event, i in events:
                event(i)

        return some

    kept, swapped = [], []
    for i in range(CHUNKS):
        t = A_FIRST + A_STEP * i
        kept += [(t, functools.partial(forward_round, more=True), i), (t + A_FAR, far_round, i)]
        t = B_FIRST + B_STEP * i
        swapped += [(t, own_round, i), (t + B_NEXT, forward_round, i), (t + B_NEXT + B_FAR, far_round, i)]
    order = lambda event: event[0]
    kept, swapped = sorted(kept, key=order), sorted(swapped, key=order)
    since = -1.0
    for s, until in enumerate(TOKEN_TIMES + (1e9,)):
        pl.when(jnp.logical_not(swaps))(run([e[1:] for e in kept if since <= e[0] < until]))
        pl.when(swaps)(run([e[1:] for e in swapped if since <= e[0] < until]))
        since = until
        if s < 4:
            token_round(s)
    for i in range(GU_CHUNKS):
        for r in range(4):
            share(i, r).wait_recv()
    for p in range(4):
        for k in range(1, 8):
            there(p, k).wait_recv()

    for k in range(1, 8):
        meta_z(k).wait_recv()
    for p in range(4):
        weigh(1, p)

    def hidden_step(s, carry):
        for m in range(2):
            rows = pl.ds(m * 256, 256)
            both = jnp.dot(ib[rows, :], gu[s], preferred_element_type=F32)
            g, u = both[:, :128], both[:, 128:]
            hid[rows, pl.ds(pl.multiple_of(s * 128, 128), 128)] = g / (1.0 + jnp.exp(-g)) * u
        return carry

    lax.fori_loop(0, 8, hidden_step, 0)
    for i in range(GU_CHUNKS, CHUNKS):
        for r in range(4):
            share(i, r).wait_recv()

    for p in (3, 2, 1, 0):
        for h in range(2):
            if h == 0:
                lhs[...] = hid[pl.ds(p * 128, 128), :].astype(BF16)
            else:
                for q in range(4):
                    first = q * 128 + p * 32
                    part = [hid[pl.ds(first + g, 8), :] for g in (0, 16, 8, 24)]
                    lhs[pl.ds(q * 32, 32), :] = jnp.concatenate(part, axis=0).astype(BF16)

            def answer_step(c, carry, h=h, p=p):
                first = pl.multiple_of(c * 256, 256)
                down = jnp.concatenate([dn[s, pl.ds(h * 1024 + first, 256), :] for s in range(8)], axis=1)
                a = lax.dot_general(lhs[...], down, (((1,), (1,)), ((), ())), preferred_element_type=F32)
                ans[h, pl.ds(p * 128, 128), pl.ds(first, 256)] = a.astype(BF16)
                return carry

            lax.fori_loop(0, 4, answer_step, 0)
            for k in Z_ORDER:
                back(h, p, k).start()
            ret[h, pl.ds(p * 128, 16), :] = ans[h, pl.ds(p * 128, 16), :]

    def sum_up(h, s):
        rows = pl.ds(0, 32 if s == 0 else 64)
        to = dev(dy=1) if h == 0 else dev(dz=1)
        return rdma(rs_out.at[h, 0, s, rows, :], rs_in.at[h, 0, s, rows, :], r_send.at[h, 0, s], r_recv.at[h, 0, s], to)

    def sum_down(h, s):
        rows = pl.ds(32, 32) if s == 0 else pl.ds(0, 64)
        to = dev(dy=-1) if h == 0 else dev(dz=-1)
        return rdma(rs_out.at[h, 1, s, rows, :], rs_in.at[h, 1, s, rows, :], r_send.at[h, 1, s], r_recv.at[h, 1, s], to)

    def combine(h, p):
        for k in range(1, 8):
            back(h, p, k).wait_recv()
        for c in range(2):
            cols = pl.ds(c * 512, 512)
            r = ret[h, pl.ds(p * 128, 128), cols]
            high = jnp.dot(wh[h, p], r, preferred_element_type=F32)
            pt[h, :, cols] = high + jnp.dot(wl[h, p], r, preferred_element_type=F32)

    def add_up(h, s, first):
        sum_up(h, s - 1).wait_recv()
        if s == 1:
            rs_out[h, 0, s, 0:32, :] = (pt[h, first : first + 32, :] + rs_in[h, 0, 0, 0:32, :].astype(F32)).astype(BF16)
            rs_out[h, 0, s, 32:64, :] = pt[h, first + 32 : first + 64, :].astype(BF16)
        else:
            rs_out[h, 0, s] = (pt[h, first : first + 64, :] + rs_in[h, 0, s - 1].astype(F32)).astype(BF16)
        sum_up(h, s).start()

    def add_down(h, s, first):
        sum_down(h, s - 1).wait_recv()
        if s == 1:
            rs_out[h, 1, s, 0:32, :] = pt[h, first : first + 32, :].astype(BF16)
            last = pt[h, first + 32 : first + 64, :] + rs_in[h, 1, 0, 32:64, :].astype(F32)
            rs_out[h, 1, s, 32:64, :] = last.astype(BF16)
        else:
            rs_out[h, 1, s] = (pt[h, first : first + 64, :] + rs_in[h, 1, s - 1].astype(F32)).astype(BF16)
        sum_down(h, s).start()

    for h in range(2):
        combine(h, 3)
        rs_out[h, 0, 0, 0:32, :] = pt[h, 64:96, :].astype(BF16)
        rs_out[h, 1, 0, 32:64, :] = pt[h, 96:128, :].astype(BF16)
        sum_up(h, 0).start()
        sum_down(h, 0).start()
    for h in range(2):
        add_up(h, 1, 0)
    for h in range(2):
        combine(h, 2)
        add_down(h, 1, 64)
        add_up(h, 2, 0)
    for h in range(2):
        combine(h, 1)
        add_down(h, 2, 64)
        add_up(h, 3, 0)
    for h in range(2):
        combine(h, 0)
        add_down(h, 3, 64)
    for h in range(2):
        sum_up(h, 3).wait_recv()
        sum_down(h, 3).wait_recv()
        total = pt[h, 0:64, :] + rs_in[h, 0, 3].astype(F32) + rs_in[h, 1, 3].astype(F32)
        o_ref[:, h * 1024 : h * 1024 + 1024] = total.astype(BF16)

    @pl.when(swaps)
    def _():
        for i in range(CHUNKS):
            swap(i).wait_send()

    for i in range(CHUNKS):
        own_up(i).wait_send()
        own_down(i).wait_send()
        on_up(i).wait_send()
        on_down(i).wait_send()
        for r in range(4):
            share(i, r).wait_send()
    for s in range(4):
        tok_up(s).wait_send()
        tok_down(s).wait_send()
        meta_up(s).wait_send()
        if s < 3:
            meta_down(s).wait_send()
        for h in range(2):
            sum_up(h, s).wait_send()
            sum_down(h, s).wait_send()
    for k in range(1, 8):
        meta_z(k).wait_send()
        for p in range(4):
            there(p, k).wait_send()
            for h in range(2):
                back(h, p, k).wait_send()


def local(
    tokens,
    route_gates,
    expert_ids,
    slot_index,
    gate_quant,
    up_quant,
    down_quant,
    gate_scale,
    up_scale,
    down_scale,
):
    y_of = (expert_ids % 2) * 4 + (expert_ids // 2) % 4
    code = jnp.where(slot_index >= 0, y_of * 64 + (expert_ids // 8) * 8 + slot_index, -1).astype(F32)
    info = jnp.concatenate([code, route_gates], axis=1).T
    info = jnp.concatenate([info, info], axis=1)
    vmem = pl.BlockSpec(memory_space=pltpu.VMEM)
    smem = pl.BlockSpec(memory_space=pltpu.SMEM)
    dma = pltpu.SemaphoreType.DMA
    return pl.pallas_call(
        kernel,
        out_shape=jax.ShapeDtypeStruct((64, 2048), BF16),
        in_specs=[vmem, vmem, smem, smem, smem, vmem, vmem, vmem],
        out_specs=vmem,
        scratch_shapes=[
            pltpu.VMEM((8, 64, 2048), BF16),
            pltpu.VMEM((8, 16, 128), F32),
            pltpu.VMEM((8, 16, 128), F32),
            pltpu.VMEM((512, 2048), BF16),
            pltpu.VMEM((512, 2048), BF16),
            pltpu.VMEM((8, 2048, 256), BF16),
            pltpu.VMEM((8, 2048, 128), BF16),
            pltpu.VMEM((2048, 256), BF16),
            pltpu.VMEM((2048, 128), BF16),
            pltpu.VMEM((512, 1024), F32),
            pltpu.VMEM((128, 1024), BF16),
            pltpu.VMEM((2, 512, 1024), BF16),
            pltpu.VMEM((2, 512, 1024), BF16),
            pltpu.VMEM((2, 4, 128, 128), BF16),
            pltpu.VMEM((2, 4, 128, 128), BF16),
            pltpu.VMEM((2, 128, 1024), F32),
            pltpu.VMEM((2, 2, 4, 64, 1024), BF16),
            pltpu.VMEM((2, 2, 4, 64, 1024), BF16),
            dma((CHUNKS, 9)),
            dma((CHUNKS, 9)),
            dma((2, 4)),
            dma((2, 4)),
            dma((2, 4)),
            dma((2, 4)),
            dma((8,)),
            dma((8,)),
            dma((4, 8)),
            dma((4, 8)),
            dma((2, 4, 8)),
            dma((2, 4, 8)),
            dma((2, 2, 4)),
            dma((2, 2, 4)),
        ],
        compiler_params=pltpu.CompilerParams(
            collective_id=0, has_side_effects=True, vmem_limit_bytes=56 * 2**20
        ),
        name="experts",
    )(
        tokens,
        info,
        gate_scale.reshape(16),
        up_scale.reshape(16),
        down_scale.reshape(16),
        gate_quant[0],
        up_quant[0],
        down_quant[0],
    )


def solution(mesh):
    return jax.shard_map(
        local,
        mesh=mesh,
        in_specs=(
            P(("stream", "expert"), None),
            P(("stream", "expert"), None),
            P(("stream", "expert"), None),
            P(("stream", "expert"), None),
            P("expert", None, "stream"),
            P("expert", None, "stream"),
            P("expert", None, "stream"),
            P("expert", None, "stream"),
            P("expert", None, "stream"),
            P("expert", None, "stream"),
        ),
        out_specs=P(("stream", "expert"), None),
        check_vma=False,
    )
```

```python
import functools

import jax
import jax.numpy as jnp
from jax import lax
from jax.experimental import pallas as pl
from jax.experimental.pallas import tpu as pltpu
from jax.sharding import PartitionSpec as P

MESH = pl.DeviceIdType.MESH
F32 = jnp.float32
BF16 = jnp.bfloat16
GU_CHUNKS = 4
DN_CHUNKS = 2
CHUNKS = GU_CHUNKS + DN_CHUNKS
TOKEN_TIMES = (8.0, 17.0, 25.0, 32.0)
PAIRS = (3, 2, 1, 0)
LATE = 1
BACK_WINDOW = 2
A_FIRST, A_STEP, A_FAR = 6.0, 4.0, 5.0
SWAP_WINDOW = 2
OWN_WINDOW = 2
B_FIRST, B_STEP, B_NEXT, B_FAR = 9.0, 7.0, 7.5, 7.0
Z_ORDER = (7, 6, 5, 4, 3, 2, 1)
OFFSETS = (0, -1, 1, -2, 2, -3, 3, 4)
UP = (0, 1, 3, 5, 7)
DOWN = (0, 2, 4, 6, 7)


def kernel(
    tok, gates, ids, slots, sg, su, sd, gq, uq, dq, o_ref,
    tk, mt, mz, ob, ib, gu, dn, lg, ld, hid, lhs, ans, ret, wh, wl, pt, rs_out, rs_in,
    w_send, w_recv, t_send, t_recv, m_send, m_recv, n_send, n_recv, a_send, a_recv, b_send, b_recv, r_send, r_recv,
):
    stream, expert = lax.axis_index("stream"), lax.axis_index("expert")
    x, y_hi = stream // 2, stream % 2
    z, y_lo, core = expert // 8, (expert % 8) // 2, expert % 2
    y = 4 * y_hi + y_lo

    def dev(dx=0, dy=0, dz=0, dc=0):
        xx, yy, zz, cc = (x + dx + 4) % 4, (y + dy + 8) % 8, (z + dz + 8) % 8, (core + dc) % 2
        return (2 * xx + yy // 4, 8 * zz + 2 * (yy % 4) + cc)

    def rdma(src, dst, send, recv, device):
        return pltpu.make_async_remote_copy(
            src_ref=src, dst_ref=dst, send_sem=send, recv_sem=recv, device_id=device, device_id_type=MESH
        )

    swaps = core != y_hi
    barrier = pltpu.get_barrier_semaphore()
    peers = [dev(dx=1), dev(dx=-1), dev(dc=1), dev(dy=4, dc=1)]
    peers += [dev(dy=k) for k in range(1, 8)] + [dev(dz=k) for k in range(1, 8)]
    for peer in peers:
        pl.semaphore_signal(barrier, inc=1, device_id=peer, device_id_type=MESH)

    def dequantize(i):
        if i < GU_CHUNKS:
            n, first = 16 // GU_CHUNKS, i * (16 // GU_CHUNKS)
        else:
            n, first = 16 // DN_CHUNKS, (i - GU_CHUNKS) * (16 // DN_CHUNKS)

        def fill(gu_ref, dn_ref):
            def block(b, carry):
                rows = pl.ds(pl.multiple_of(b * 128, 128), 128)
                if i < GU_CHUNKS:
                    gu_ref[rows, 0:128] = (gq[rows, :].astype(F32) * sg[b]).astype(BF16)
                    gu_ref[rows, 128:256] = (uq[rows, :].astype(F32) * su[b]).astype(BF16)
                else:
                    dn_ref[rows, :] = (dq[rows, :].astype(F32) * sd[b]).astype(BF16)
                return carry

            lax.fori_loop(first, first + n, block, 0)

        pl.when(swaps)(lambda: fill(lg, ld))
        pl.when(jnp.logical_not(swaps))(lambda: fill(gu.at[0], dn.at[0]))

    tk[0] = tok[...]
    chosen, place = ids[...], slots[...]
    code = ((chosen % 2) * 4 + (chosen // 2) % 4) * 64 + (chosen // 8) * 8 + place
    code = jnp.where(place >= 0, code, -1).astype(F32)
    info = jnp.concatenate([code, gates[...]], axis=0)
    info = jnp.concatenate([info, info], axis=1)
    mt[0] = info
    mz[0] = info
    for i in range(CHUNKS):
        dequantize(i)
    pl.semaphore_wait(barrier, len(peers))

    def piece(slot, i, part=None):
        if i < GU_CHUNKS:
            rows = 2048 // GU_CHUNKS
            first = i * rows
        else:
            rows = 2048 // DN_CHUNKS
            first = (i - GU_CHUNKS) * rows
        if part is not None:
            rows //= 2
            first += part * rows
        if i < GU_CHUNKS:
            return gu.at[slot, pl.ds(first, rows), :]
        return dn.at[slot, pl.ds(first, rows), :]

    def local_piece(i):
        if i < GU_CHUNKS:
            rows = 2048 // GU_CHUNKS
            return lg.at[pl.ds(i * rows, rows), :]
        rows = 2048 // DN_CHUNKS
        return ld.at[pl.ds((i - GU_CHUNKS) * rows, rows), :]

    def swap(i):
        return rdma(local_piece(i), piece(0, i), w_send.at[i, 0], w_recv.at[i, 0], dev(dy=4, dc=1))

    def own_up(i):
        return rdma(piece(0, i), piece(6, i), w_send.at[i, 1], w_recv.at[i, 1], dev(dx=1))

    def own_down(i):
        return rdma(piece(0, i), piece(2, i), w_send.at[i, 2], w_recv.at[i, 2], dev(dx=-1))

    def on_up(i):
        return rdma(piece(6, i, 0), piece(4, i, 0), w_send.at[i, 3], w_recv.at[i, 3], dev(dx=1))

    def on_down(i):
        return rdma(piece(2, i, 1), piece(4, i, 1), w_send.at[i, 4], w_recv.at[i, 4], dev(dx=-1))

    def share(i, r):
        return rdma(piece(2 * r, i), piece(2 * r + 1, i), w_send.at[i, 5 + r], w_recv.at[i, 5 + r], dev(dc=1))

    def tok_up(s):
        src, dst = tk.at[UP[s]], tk.at[UP[s + 1]]
        if s == 3:
            src, dst = src.at[pl.ds(0, 32), :], dst.at[pl.ds(0, 32), :]
        return rdma(src, dst, t_send.at[0, s], t_recv.at[0, s], dev(dy=1))

    def tok_down(s):
        src, dst = tk.at[DOWN[s]], tk.at[DOWN[s + 1]]
        if s == 3:
            src, dst = src.at[pl.ds(32, 32), :], dst.at[pl.ds(32, 32), :]
        return rdma(src, dst, t_send.at[1, s], t_recv.at[1, s], dev(dy=-1))

    def meta_up(s):
        return rdma(mt.at[UP[s]], mt.at[UP[s + 1]], m_send.at[0, s], m_recv.at[0, s], dev(dy=1))

    def meta_down(s):
        return rdma(mt.at[DOWN[s]], mt.at[DOWN[s + 1]], m_send.at[1, s], m_recv.at[1, s], dev(dy=-1))

    def token_start(s):
        tok_up(s).start()
        tok_down(s).start()
        meta_up(s).start()
        if s < 3:
            meta_down(s).start()

    def token_arrived(s):
        tok_up(s).wait_recv()
        tok_down(s).wait_recv()
        meta_up(s).wait_recv()
        if s < 3:
            meta_down(s).wait_recv()

    def meta_z(k):
        return rdma(mt.at[0], mz.at[k], n_send.at[k], n_recv.at[k], dev(dz=-OFFSETS[k]))

    def there(p, k):
        rows = pl.ds(p * 128 + k * 16, 16)
        return rdma(ob.at[rows, :], ib.at[rows, :], a_send.at[p, k], a_recv.at[p, k], dev(dz=-OFFSETS[k]))

    def back(h, p, k):
        rows = pl.ds(p * 128 + k * 16, 16)
        to = dev(dz=OFFSETS[k]) if h == 0 else dev(dy=OFFSETS[k])
        return rdma(ans.at[h, rows, :], ret.at[h, rows, :], b_send.at[h, p, k], b_recv.at[h, p, k], to)

    def weigh(h, p):
        gathered = mt if h == 0 else mz
        row = lax.broadcasted_iota(jnp.int32, (128, 128), 0)
        lane = lax.broadcasted_iota(jnp.int32, (128, 128), 1)
        block = row // 16
        off = jnp.where(block % 2 == 1, -((block + 1) // 2), block // 2)
        if h == 0:
            target = y * 64 + ((z - off + 8) % 8) * 8 + row % 8
        else:
            target = ((y - off + 8) % 8) * 64 + z * 8 + row % 8
        target = jnp.where((row % 16) // 8 == lane // 64, target, -5).astype(F32)
        half = lax.broadcasted_iota(jnp.int32, (16, 128), 1) // 64
        info = jnp.where(half == 0, gathered[2 * p], gathered[2 * p + 1])
        hit = jnp.zeros((128, 128), F32)
        weight = jnp.zeros((128, 128), F32)
        for k in range(8):
            same = target == info[k : k + 1, :]
            hit = jnp.where(same, 1.0, hit)
            weight = jnp.where(same, info[8 + k : 9 + k, :], weight)
        weight = weight.T
        high = weight.astype(BF16)
        wh[h, p] = high
        wl[h, p] = (weight - high.astype(F32)).astype(BF16)
        return hit.astype(BF16)

    def dispatch(p):
        hit = weigh(0, p)
        for c in range(4):
            cols = pl.ds(c * 512, 512)
            both = jnp.concatenate([tk[2 * p, :, cols], tk[2 * p + 1, :, cols]], axis=0)
            ob[pl.ds(p * 128, 128), cols] = jnp.dot(hit, both, preferred_element_type=F32).astype(BF16)
        for k in Z_ORDER:
            there(p, k).start()
        ib[pl.ds(p * 128, 16), :] = ob[pl.ds(p * 128, 16), :]

    def own_start(i):
        own_up(i).start()
        own_down(i).start()
        share(i, 0).start()

    token_start(0)
    for k in range(1, 8):
        meta_z(k).start()

    @pl.when(swaps)
    def _():
        for i in range(SWAP_WINDOW):
            swap(i).start()

    @pl.when(jnp.logical_not(swaps))
    def _():
        for i in range(OWN_WINDOW):
            own_start(i)

    def own_round(i):
        swap(i).wait_recv()
        if i + SWAP_WINDOW < CHUNKS:
            swap(i + SWAP_WINDOW).start()
        own_start(i)

    def forward_round(i, more=False):
        own_up(i).wait_recv()
        on_up(i).start()
        own_down(i).wait_recv()
        on_down(i).start()
        if more and i + OWN_WINDOW < CHUNKS:
            own_start(i + OWN_WINDOW)
        share(i, 3).start()
        share(i, 1).start()

    def far_round(i):
        on_up(i).wait_recv()
        on_down(i).wait_recv()
        share(i, 2).start()

    def token_round(s):
        token_arrived(s)
        if s < 3:
            token_start(s + 1)
        dispatch(s)

    def run(events):
        def some():
            for event, i in events:
                event(i)

        return some

    kept, swapped = [], []
    for i in range(CHUNKS):
        t = A_FIRST + A_STEP * i
        kept += [(t, functools.partial(forward_round, more=True), i), (t + A_FAR, far_round, i)]
        t = B_FIRST + B_STEP * i
        swapped += [(t, own_round, i), (t + B_NEXT, forward_round, i), (t + B_NEXT + B_FAR, far_round, i)]
    order = lambda event: event[0]
    kept, swapped = sorted(kept, key=order), sorted(swapped, key=order)
    def part(events, since, until):
        return run([e[1:] for e in events if since <= e[0] < until])

    late = [(forward_round, CHUNKS - 1), (far_round, CHUNKS - 1)][2 - LATE :]
    swapped = [e for e in swapped if e[1:] not in late]
    times = (-1.0,) + TOKEN_TIMES + (1e9,)
    for s in range(5):
        pl.when(jnp.logical_not(swaps))(part(kept, times[s], times[s + 1]))
        pl.when(swaps)(part(swapped, times[s], times[s + 1]))
        if s == 3:
            for k in range(1, 8):
                meta_z(k).wait_recv()
            for p in range(4):
                weigh(1, p)
        if s < 4:
            token_round(s)

    def hidden(m, since, until):
        def hidden_step(s, carry):
            rows = pl.ds(m * 256, 256)
            both = jnp.dot(ib[rows, :], gu[s], preferred_element_type=F32)
            g, u = both[:, :128], both[:, 128:]
            hid[rows, pl.ds(pl.multiple_of(s * 128, 128), 128)] = g / (1.0 + jnp.exp(-g)) * u
            return carry

        for p in (2 * m, 2 * m + 1):
            if since == 0:
                for k in range(1, 8):
                    there(p, k).wait_recv()
        lax.fori_loop(since, until, hidden_step, 0)

    for i in range(GU_CHUNKS):
        for r in range(4):
            share(i, r).wait_recv()
    hidden(0, 0, 4)
    pl.when(swaps)(run(late[:-1]))
    hidden(0, 4, 8)
    pl.when(swaps)(run(late[-1:]))
    hidden(1, 0, 8)

    for h in range(2):
        for i in range(GU_CHUNKS + h * (DN_CHUNKS // 2), GU_CHUNKS + (h + 1) * (DN_CHUNKS // 2)):
            for r in range(4):
                share(i, r).wait_recv()
        for p in range(4):
            if h == 0:
                lhs[pl.ds(p * 128, 128), :] = hid[pl.ds(p * 128, 128), :].astype(BF16)
            else:
                for q in range(4):
                    first = q * 128 + p * 32
                    some = [hid[pl.ds(first + g, 8), :] for g in (0, 16, 8, 24)]
                    lhs[pl.ds(p * 128 + q * 32, 32), :] = jnp.concatenate(some, axis=0).astype(BF16)

        def answer_step(c, carry, h=h):
            first = pl.multiple_of(c * 256, 256)
            down = jnp.concatenate([dn[s, pl.ds(h * 1024 + first, 256), :] for s in range(8)], axis=1)
            for m in range(2):
                rows = pl.ds(m * 256, 256)
                a = lax.dot_general(lhs[rows, :], down, (((1,), (1,)), ((), ())), preferred_element_type=F32)
                ans[h, rows, pl.ds(first, 256)] = a.astype(BF16)
            return carry

        lax.fori_loop(0, 4, answer_step, 0)
        for p in range(4):
            ret[h, pl.ds(p * 128, 16), :] = ans[h, pl.ds(p * 128, 16), :]
        for p in PAIRS[:BACK_WINDOW]:
            for k in Z_ORDER:
                back(h, p, k).start()

    def sum_up(h, s):
        rows = pl.ds(0, 32 if s == 0 else 64)
        to = dev(dy=1) if h == 0 else dev(dz=1)
        return rdma(rs_out.at[h, 0, s, rows, :], rs_in.at[h, 0, s, rows, :], r_send.at[h, 0, s], r_recv.at[h, 0, s], to)

    def sum_down(h, s):
        rows = pl.ds(32, 32) if s == 0 else pl.ds(0, 64)
        to = dev(dy=-1) if h == 0 else dev(dz=-1)
        return rdma(rs_out.at[h, 1, s, rows, :], rs_in.at[h, 1, s, rows, :], r_send.at[h, 1, s], r_recv.at[h, 1, s], to)

    def combine(h, p):
        for k in range(1, 8):
            back(h, p, k).wait_recv()
        for later in PAIRS[PAIRS.index(p) + BACK_WINDOW :][:1]:
            for k in Z_ORDER:
                back(h, later, k).start()
        for c in range(2):
            cols = pl.ds(c * 512, 512)
            r = ret[h, pl.ds(p * 128, 128), cols]
            high = jnp.dot(wh[h, p], r, preferred_element_type=F32)
            pt[h, :, cols] = high + jnp.dot(wl[h, p], r, preferred_element_type=F32)

    def add_up(h, s, first):
        sum_up(h, s - 1).wait_recv()
        if s == 1:
            rs_out[h, 0, s, 0:32, :] = (pt[h, first : first + 32, :] + rs_in[h, 0, 0, 0:32, :].astype(F32)).astype(BF16)
            rs_out[h, 0, s, 32:64, :] = pt[h, first + 32 : first + 64, :].astype(BF16)
        else:
            rs_out[h, 0, s] = (pt[h, first : first + 64, :] + rs_in[h, 0, s - 1].astype(F32)).astype(BF16)
        sum_up(h, s).start()

    def add_down(h, s, first):
        sum_down(h, s - 1).wait_recv()
        if s == 1:
            rs_out[h, 1, s, 0:32, :] = pt[h, first : first + 32, :].astype(BF16)
            last = pt[h, first + 32 : first + 64, :] + rs_in[h, 1, 0, 32:64, :].astype(F32)
            rs_out[h, 1, s, 32:64, :] = last.astype(BF16)
        else:
            rs_out[h, 1, s] = (pt[h, first : first + 64, :] + rs_in[h, 1, s - 1].astype(F32)).astype(BF16)
        sum_down(h, s).start()

    for h in range(2):
        combine(h, 3)
        rs_out[h, 0, 0, 0:32, :] = pt[h, 64:96, :].astype(BF16)
        rs_out[h, 1, 0, 32:64, :] = pt[h, 96:128, :].astype(BF16)
        sum_up(h, 0).start()
        sum_down(h, 0).start()
    for h in range(2):
        add_up(h, 1, 0)
    for h in range(2):
        combine(h, 2)
        add_down(h, 1, 64)
        add_up(h, 2, 0)
    for h in range(2):
        combine(h, 1)
        add_down(h, 2, 64)
        add_up(h, 3, 0)
    for h in range(2):
        combine(h, 0)
        add_down(h, 3, 64)
    for h in range(2):
        sum_up(h, 3).wait_recv()
        sum_down(h, 3).wait_recv()
        total = pt[h, 0:64, :] + rs_in[h, 0, 3].astype(F32) + rs_in[h, 1, 3].astype(F32)
        o_ref[:, h * 1024 : h * 1024 + 1024] = total.astype(BF16)

    @pl.when(swaps)
    def _():
        for i in range(CHUNKS):
            swap(i).wait_send()

    for i in range(CHUNKS):
        own_up(i).wait_send()
        own_down(i).wait_send()
        on_up(i).wait_send()
        on_down(i).wait_send()
        for r in range(4):
            share(i, r).wait_send()
    for s in range(4):
        tok_up(s).wait_send()
        tok_down(s).wait_send()
        meta_up(s).wait_send()
        if s < 3:
            meta_down(s).wait_send()
        for h in range(2):
            sum_up(h, s).wait_send()
            sum_down(h, s).wait_send()
    for k in range(1, 8):
        meta_z(k).wait_send()
        for p in range(4):
            there(p, k).wait_send()
            for h in range(2):
                back(h, p, k).wait_send()


def local(
    tokens,
    route_gates,
    expert_ids,
    slot_index,
    gate_quant,
    up_quant,
    down_quant,
    gate_scale,
    up_scale,
    down_scale,
):
    vmem = pl.BlockSpec(memory_space=pltpu.VMEM)
    smem = pl.BlockSpec(memory_space=pltpu.SMEM)
    dma = pltpu.SemaphoreType.DMA
    return pl.pallas_call(
        kernel,
        out_shape=jax.ShapeDtypeStruct((64, 2048), BF16),
        in_specs=[vmem] * 4 + [smem] * 3 + [vmem] * 3,
        out_specs=vmem,
        scratch_shapes=[
            pltpu.VMEM((8, 64, 2048), BF16),
            pltpu.VMEM((8, 16, 128), F32),
            pltpu.VMEM((8, 16, 128), F32),
            pltpu.VMEM((512, 2048), BF16),
            pltpu.VMEM((512, 2048), BF16),
            pltpu.VMEM((8, 2048, 256), BF16),
            pltpu.VMEM((8, 2048, 128), BF16),
            pltpu.VMEM((2048, 256), BF16),
            pltpu.VMEM((2048, 128), BF16),
            pltpu.VMEM((512, 1024), F32),
            pltpu.VMEM((512, 1024), BF16),
            pltpu.VMEM((2, 512, 1024), BF16),
            pltpu.VMEM((2, 512, 1024), BF16),
            pltpu.VMEM((2, 4, 128, 128), BF16),
            pltpu.VMEM((2, 4, 128, 128), BF16),
            pltpu.VMEM((2, 128, 1024), F32),
            pltpu.VMEM((2, 2, 4, 64, 1024), BF16),
            pltpu.VMEM((2, 2, 4, 64, 1024), BF16),
            dma((CHUNKS, 9)),
            dma((CHUNKS, 9)),
            dma((2, 4)),
            dma((2, 4)),
            dma((2, 4)),
            dma((2, 4)),
            dma((8,)),
            dma((8,)),
            dma((4, 8)),
            dma((4, 8)),
            dma((2, 4, 8)),
            dma((2, 4, 8)),
            dma((2, 2, 4)),
            dma((2, 2, 4)),
        ],
        compiler_params=pltpu.CompilerParams(
            collective_id=0, has_side_effects=True, vmem_limit_bytes=56 * 2**20
        ),
        name="experts",
    )(
        tokens,
        route_gates.T,
        expert_ids.T,
        slot_index.T,
        gate_scale.reshape(16),
        up_scale.reshape(16),
        down_scale.reshape(16),
        gate_quant[0],
        up_quant[0],
        down_quant[0],
    )


def solution(mesh):
    return jax.shard_map(
        local,
        mesh=mesh,
        in_specs=(
            P(("stream", "expert"), None),
            P(("stream", "expert"), None),
            P(("stream", "expert"), None),
            P(("stream", "expert"), None),
            P("expert", None, "stream"),
            P("expert", None, "stream"),
            P("expert", None, "stream"),
            P("expert", None, "stream"),
            P("expert", None, "stream"),
            P("expert", None, "stream"),
        ),
        out_specs=P(("stream", "expert"), None),
        check_vma=False,
    )
```

```python
import functools

import jax
import jax.numpy as jnp
from jax import lax
from jax.experimental import pallas as pl
from jax.experimental.pallas import tpu as pltpu
from jax.sharding import PartitionSpec as P

MESH = pl.DeviceIdType.MESH
F32 = jnp.float32
BF16 = jnp.bfloat16
GU_CHUNKS = 4
DN_CHUNKS = 2
CHUNKS = GU_CHUNKS + DN_CHUNKS
TOKEN_TIMES = (8.0, 17.0, 25.0, 32.0)
PAIRS = (3, 2, 1, 0)
LATE = 1
BACK_WINDOW = 2
A_FIRST, A_STEP, A_FAR = 6.0, 4.0, 5.0
SWAP_WINDOW = 2
OWN_WINDOW = 2
B_FIRST, B_STEP, B_NEXT, B_FAR = 9.0, 7.0, 7.5, 7.0
Z_ORDER = (7, 6, 5, 4, 3, 2, 1)
OFFSETS = (0, -1, 1, -2, 2, -3, 3, 4)
UP = (0, 1, 3, 5, 7)
DOWN = (0, 2, 4, 6, 7)


def kernel(
    tok, gates, ids, slots, sg, su, sd, gq, uq, dq, o_ref,
    tk, mt, mz, ob, ib, gu, dn, lg, ld, hid, lhs, ans, ret, wh, wl, pt, rs_out, rs_in,
    w_send, w_recv, t_send, t_recv, m_send, m_recv, n_send, n_recv, a_send, a_recv, b_send, b_recv, r_send, r_recv,
):
    stream, expert = lax.axis_index("stream"), lax.axis_index("expert")
    x, y_hi = stream // 2, stream % 2
    z, y_lo, core = expert // 8, (expert % 8) // 2, expert % 2
    y = 4 * y_hi + y_lo

    def dev(dx=0, dy=0, dz=0, dc=0):
        xx, yy, zz, cc = (x + dx + 4) % 4, (y + dy + 8) % 8, (z + dz + 8) % 8, (core + dc) % 2
        return (2 * xx + yy // 4, 8 * zz + 2 * (yy % 4) + cc)

    def rdma(src, dst, send, recv, device):
        return pltpu.make_async_remote_copy(
            src_ref=src, dst_ref=dst, send_sem=send, recv_sem=recv, device_id=device, device_id_type=MESH
        )

    swaps = core != y_hi
    barrier = pltpu.get_barrier_semaphore()
    peers = [dev(dx=1), dev(dx=-1), dev(dc=1), dev(dy=4, dc=1)]
    peers += [dev(dy=k) for k in range(1, 8)] + [dev(dz=k) for k in range(1, 8)]
    for peer in peers:
        pl.semaphore_signal(barrier, inc=1, device_id=peer, device_id_type=MESH)

    def dequantize(i):
        if i < GU_CHUNKS:
            n, first = 16 // GU_CHUNKS, i * (16 // GU_CHUNKS)
        else:
            n, first = 16 // DN_CHUNKS, (i - GU_CHUNKS) * (16 // DN_CHUNKS)

        def fill(gu_ref, dn_ref):
            def block(b, carry):
                rows = pl.ds(pl.multiple_of(b * 128, 128), 128)
                if i < GU_CHUNKS:
                    gu_ref[rows, 0:128] = (gq[rows, :].astype(F32) * sg[b]).astype(BF16)
                    gu_ref[rows, 128:256] = (uq[rows, :].astype(F32) * su[b]).astype(BF16)
                else:
                    dn_ref[rows, :] = (dq[rows, :].astype(F32) * sd[b]).astype(BF16)
                return carry

            lax.fori_loop(first, first + n, block, 0)

        pl.when(swaps)(lambda: fill(lg, ld))
        pl.when(jnp.logical_not(swaps))(lambda: fill(gu.at[0], dn.at[0]))

    tk[0] = tok[...]
    chosen, place = ids[...], slots[...]
    code = ((chosen % 2) * 4 + (chosen // 2) % 4) * 64 + (chosen // 8) * 8 + place
    code = jnp.where(place >= 0, code, -1).astype(F32)
    info = jnp.concatenate([code, gates[...]], axis=0)
    info = jnp.concatenate([info, info], axis=1)
    mt[0] = info
    mz[0] = info
    for i in range(CHUNKS):
        dequantize(i)
    pl.semaphore_wait(barrier, len(peers))

    def piece(slot, i, part=None):
        if i < GU_CHUNKS:
            rows = 2048 // GU_CHUNKS
            first = i * rows
        else:
            rows = 2048 // DN_CHUNKS
            first = (i - GU_CHUNKS) * rows
        if part is not None:
            rows //= 2
            first += part * rows
        if i < GU_CHUNKS:
            return gu.at[slot, pl.ds(first, rows), :]
        return dn.at[slot, pl.ds(first, rows), :]

    def local_piece(i):
        if i < GU_CHUNKS:
            rows = 2048 // GU_CHUNKS
            return lg.at[pl.ds(i * rows, rows), :]
        rows = 2048 // DN_CHUNKS
        return ld.at[pl.ds((i - GU_CHUNKS) * rows, rows), :]

    def swap(i):
        return rdma(local_piece(i), piece(0, i), w_send.at[i, 0], w_recv.at[i, 0], dev(dy=4, dc=1))

    def own_up(i):
        return rdma(piece(0, i), piece(6, i), w_send.at[i, 1], w_recv.at[i, 1], dev(dx=1))

    def own_down(i):
        return rdma(piece(0, i), piece(2, i), w_send.at[i, 2], w_recv.at[i, 2], dev(dx=-1))

    def on_up(i):
        return rdma(piece(6, i, 0), piece(4, i, 0), w_send.at[i, 3], w_recv.at[i, 3], dev(dx=1))

    def on_down(i):
        return rdma(piece(2, i, 1), piece(4, i, 1), w_send.at[i, 4], w_recv.at[i, 4], dev(dx=-1))

    def share(i, r):
        return rdma(piece(2 * r, i), piece(2 * r + 1, i), w_send.at[i, 5 + r], w_recv.at[i, 5 + r], dev(dc=1))

    def tok_up(s):
        src, dst = tk.at[UP[s]], tk.at[UP[s + 1]]
        if s == 3:
            src, dst = src.at[pl.ds(0, 32), :], dst.at[pl.ds(0, 32), :]
        return rdma(src, dst, t_send.at[0, s], t_recv.at[0, s], dev(dy=1))

    def tok_down(s):
        src, dst = tk.at[DOWN[s]], tk.at[DOWN[s + 1]]
        if s == 3:
            src, dst = src.at[pl.ds(32, 32), :], dst.at[pl.ds(32, 32), :]
        return rdma(src, dst, t_send.at[1, s], t_recv.at[1, s], dev(dy=-1))

    def meta_up(s):
        return rdma(mt.at[UP[s]], mt.at[UP[s + 1]], m_send.at[0, s], m_recv.at[0, s], dev(dy=1))

    def meta_down(s):
        return rdma(mt.at[DOWN[s]], mt.at[DOWN[s + 1]], m_send.at[1, s], m_recv.at[1, s], dev(dy=-1))

    def token_start(s):
        tok_up(s).start()
        tok_down(s).start()
        meta_up(s).start()
        if s < 3:
            meta_down(s).start()

    def token_arrived(s):
        tok_up(s).wait_recv()
        tok_down(s).wait_recv()
        meta_up(s).wait_recv()
        if s < 3:
            meta_down(s).wait_recv()

    def meta_z(k):
        return rdma(mt.at[0], mz.at[k], n_send.at[k], n_recv.at[k], dev(dz=-OFFSETS[k]))

    def there(p, k):
        rows = pl.ds(p * 128 + k * 16, 16)
        return rdma(ob.at[rows, :], ib.at[rows, :], a_send.at[p, k], a_recv.at[p, k], dev(dz=-OFFSETS[k]))

    def back(h, p, k):
        rows = pl.ds(p * 128 + k * 16, 16)
        to = dev(dz=OFFSETS[k]) if h == 0 else dev(dy=OFFSETS[k])
        return rdma(ans.at[h, rows, :], ret.at[h, rows, :], b_send.at[h, p, k], b_recv.at[h, p, k], to)

    def weigh(h, p):
        gathered = mt if h == 0 else mz
        row = lax.broadcasted_iota(jnp.int32, (128, 128), 0)
        lane = lax.broadcasted_iota(jnp.int32, (128, 128), 1)
        block = row // 16
        off = jnp.where(block % 2 == 1, -((block + 1) // 2), block // 2)
        if h == 0:
            target = y * 64 + ((z - off + 8) % 8) * 8 + row % 8
        else:
            target = ((y - off + 8) % 8) * 64 + z * 8 + row % 8
        target = jnp.where((row % 16) // 8 == lane // 64, target, -5).astype(F32)
        half = lax.broadcasted_iota(jnp.int32, (16, 128), 1) // 64
        info = jnp.where(half == 0, gathered[2 * p], gathered[2 * p + 1])
        hit = jnp.zeros((128, 128), F32)
        weight = jnp.zeros((128, 128), F32)
        for k in range(8):
            same = target == info[k : k + 1, :]
            hit = jnp.where(same, 1.0, hit)
            weight = jnp.where(same, info[8 + k : 9 + k, :], weight)
        weight = weight.T
        high = weight.astype(BF16)
        wh[h, p] = high
        wl[h, p] = (weight - high.astype(F32)).astype(BF16)
        return hit.astype(BF16)

    def dispatch(p):
        hit = weigh(0, p)
        for c in range(4):
            cols = pl.ds(c * 512, 512)
            both = jnp.concatenate([tk[2 * p, :, cols], tk[2 * p + 1, :, cols]], axis=0)
            ob[pl.ds(p * 128, 128), cols] = jnp.dot(hit, both, preferred_element_type=F32).astype(BF16)
        for k in Z_ORDER:
            there(p, k).start()
        ib[pl.ds(p * 128, 16), :] = ob[pl.ds(p * 128, 16), :]

    def own_start(i):
        own_up(i).start()
        own_down(i).start()
        share(i, 0).start()

    token_start(0)
    for k in range(1, 8):
        meta_z(k).start()

    @pl.when(swaps)
    def _():
        for i in range(SWAP_WINDOW):
            swap(i).start()

    @pl.when(jnp.logical_not(swaps))
    def _():
        for i in range(OWN_WINDOW):
            own_start(i)

    def own_round(i):
        swap(i).wait_recv()
        if i + SWAP_WINDOW < CHUNKS:
            swap(i + SWAP_WINDOW).start()
        own_start(i)

    def forward_round(i, more=False):
        own_up(i).wait_recv()
        on_up(i).start()
        own_down(i).wait_recv()
        on_down(i).start()
        if more and i + OWN_WINDOW < CHUNKS:
            own_start(i + OWN_WINDOW)
        share(i, 3).start()
        share(i, 1).start()

    def far_round(i):
        on_up(i).wait_recv()
        on_down(i).wait_recv()
        share(i, 2).start()

    def token_round(s):
        token_arrived(s)
        if s < 3:
            token_start(s + 1)
        dispatch(s)

    def run(events):
        def some():
            for event, i in events:
                event(i)

        return some

    kept, swapped = [], []
    for i in range(CHUNKS):
        t = A_FIRST + A_STEP * i
        kept += [(t, functools.partial(forward_round, more=True), i), (t + A_FAR, far_round, i)]
        t = B_FIRST + B_STEP * i
        swapped += [(t, own_round, i), (t + B_NEXT, forward_round, i), (t + B_NEXT + B_FAR, far_round, i)]
    order = lambda event: event[0]
    kept, swapped = sorted(kept, key=order), sorted(swapped, key=order)
    def part(events, since, until):
        return run([e[1:] for e in events if since <= e[0] < until])

    late = [(forward_round, CHUNKS - 1), (far_round, CHUNKS - 1)][2 - LATE :]
    swapped = [e for e in swapped if e[1:] not in late]
    times = (-1.0,) + TOKEN_TIMES + (1e9,)
    for s in range(5):
        pl.when(jnp.logical_not(swaps))(part(kept, times[s], times[s + 1]))
        pl.when(swaps)(part(swapped, times[s], times[s + 1]))
        if s == 3:
            for k in range(1, 8):
                meta_z(k).wait_recv()
            for p in range(4):
                weigh(1, p)
        if s < 4:
            token_round(s)

    def hidden(m, since, until):
        def hidden_step(s, carry):
            rows = pl.ds(m * 256, 256)
            both = jnp.dot(ib[rows, :], gu[s], preferred_element_type=F32)
            g, u = both[:, :128], both[:, 128:]
            hid[rows, pl.ds(pl.multiple_of(s * 128, 128), 128)] = g / (1.0 + jnp.exp(-g)) * u
            return carry

        for p in (2 * m, 2 * m + 1):
            if since == 0:
                for k in range(1, 8):
                    there(p, k).wait_recv()
        lax.fori_loop(since, until, hidden_step, 0)

    for i in range(GU_CHUNKS):
        for r in range(4):
            share(i, r).wait_recv()
    hidden(0, 0, 4)
    pl.when(swaps)(run(late[:-1]))
    hidden(0, 4, 8)
    pl.when(swaps)(run(late[-1:]))
    hidden(1, 0, 8)

    for m, h in ((1, 0), (1, 1), (0, 0), (0, 1)):
        if m == 1:
            for i in range(GU_CHUNKS + h * (DN_CHUNKS // 2), GU_CHUNKS + (h + 1) * (DN_CHUNKS // 2)):
                for r in range(4):
                    share(i, r).wait_recv()
        for p in (2 * m, 2 * m + 1):
            if h == 0:
                lhs[pl.ds((p % 2) * 128, 128), :] = hid[pl.ds(p * 128, 128), :].astype(BF16)
            else:
                for q in range(4):
                    first = q * 128 + p * 32
                    some = [hid[pl.ds(first + g, 8), :] for g in (0, 16, 8, 24)]
                    lhs[pl.ds((p % 2) * 128 + q * 32, 32), :] = jnp.concatenate(some, axis=0).astype(BF16)

        def answer_step(c, carry, h=h, m=m):
            first = pl.multiple_of(c * 256, 256)
            down = jnp.concatenate([dn[s, pl.ds(h * 1024 + first, 256), :] for s in range(8)], axis=1)
            a = lax.dot_general(lhs[...], down, (((1,), (1,)), ((), ())), preferred_element_type=F32)
            ans[h, pl.ds(m * 256, 256), pl.ds(first, 256)] = a.astype(BF16)
            return carry

        lax.fori_loop(0, 4, answer_step, 0)
        for p in (2 * m + 1, 2 * m):
            ret[h, pl.ds(p * 128, 16), :] = ans[h, pl.ds(p * 128, 16), :]
            if PAIRS.index(p) < BACK_WINDOW:
                for k in Z_ORDER:
                    back(h, p, k).start()

    def sum_up(h, s):
        rows = pl.ds(0, 32 if s == 0 else 64)
        to = dev(dy=1) if h == 0 else dev(dz=1)
        return rdma(rs_out.at[h, 0, s, rows, :], rs_in.at[h, 0, s, rows, :], r_send.at[h, 0, s], r_recv.at[h, 0, s], to)

    def sum_down(h, s):
        rows = pl.ds(32, 32) if s == 0 else pl.ds(0, 64)
        to = dev(dy=-1) if h == 0 else dev(dz=-1)
        return rdma(rs_out.at[h, 1, s, rows, :], rs_in.at[h, 1, s, rows, :], r_send.at[h, 1, s], r_recv.at[h, 1, s], to)

    def combine(h, p):
        for k in range(1, 8):
            back(h, p, k).wait_recv()
        for later in PAIRS[PAIRS.index(p) + BACK_WINDOW :][:1]:
            for k in Z_ORDER:
                back(h, later, k).start()
        for c in range(2):
            cols = pl.ds(c * 512, 512)
            r = ret[h, pl.ds(p * 128, 128), cols]
            high = jnp.dot(wh[h, p], r, preferred_element_type=F32)
            pt[h, p, :, cols] = high + jnp.dot(wl[h, p], r, preferred_element_type=F32)

    def add_up(h, s, p):
        sum_up(h, s - 1).wait_recv()
        if s == 1:
            rs_out[h, 0, s, 0:32, :] = (pt[h, p, 0:32, :] + rs_in[h, 0, 0, 0:32, :].astype(F32)).astype(BF16)
            rs_out[h, 0, s, 32:64, :] = pt[h, p, 32:64, :].astype(BF16)
        else:
            rs_out[h, 0, s] = (pt[h, p, 0:64, :] + rs_in[h, 0, s - 1].astype(F32)).astype(BF16)
        sum_up(h, s).start()

    def add_down(h, s, p):
        sum_down(h, s - 1).wait_recv()
        if s == 1:
            rs_out[h, 1, s, 0:32, :] = pt[h, p, 64:96, :].astype(BF16)
            last = pt[h, p, 96:128, :] + rs_in[h, 1, 0, 32:64, :].astype(F32)
            rs_out[h, 1, s, 32:64, :] = last.astype(BF16)
        else:
            rs_out[h, 1, s] = (pt[h, p, 64:128, :] + rs_in[h, 1, s - 1].astype(F32)).astype(BF16)
        sum_down(h, s).start()

    def gathers_sent():
        @pl.when(swaps)
        def _():
            for i in range(CHUNKS):
                swap(i).wait_send()

        for i in range(CHUNKS):
            own_up(i).wait_send()
            own_down(i).wait_send()
            on_up(i).wait_send()
            on_down(i).wait_send()
            for r in range(4):
                share(i, r).wait_send()
        for s in range(4):
            tok_up(s).wait_send()
            tok_down(s).wait_send()
            meta_up(s).wait_send()
            if s < 3:
                meta_down(s).wait_send()
        for k in range(1, 8):
            meta_z(k).wait_send()
            for p in range(4):
                there(p, k).wait_send()

    for h in range(2):
        combine(h, 3)
        rs_out[h, 0, 0, 0:32, :] = pt[h, 3, 64:96, :].astype(BF16)
        rs_out[h, 1, 0, 32:64, :] = pt[h, 3, 96:128, :].astype(BF16)
        sum_up(h, 0).start()
        sum_down(h, 0).start()
    for s, p in ((1, 2), (2, 1), (3, 0)):
        for h in range(2):
            combine(h, p)
            add_down(h, s, p)
            add_up(h, s, p + 1)
        if s == 2:
            gathers_sent()
    for h in range(2):
        sum_up(h, 3).wait_recv()
        sum_down(h, 3).wait_recv()
        total = pt[h, 0, 0:64, :] + rs_in[h, 0, 3].astype(F32) + rs_in[h, 1, 3].astype(F32)
        o_ref[:, h * 1024 : h * 1024 + 1024] = total.astype(BF16)

    for h in range(2):
        for s in range(4):
            sum_up(h, s).wait_send()
            sum_down(h, s).wait_send()
        for p in range(4):
            for k in range(1, 8):
                back(h, p, k).wait_send()


def local(
    tokens,
    route_gates,
    expert_ids,
    slot_index,
    gate_quant,
    up_quant,
    down_quant,
    gate_scale,
    up_scale,
    down_scale,
):
    vmem = pl.BlockSpec(memory_space=pltpu.VMEM)
    smem = pl.BlockSpec(memory_space=pltpu.SMEM)
    dma = pltpu.SemaphoreType.DMA
    return pl.pallas_call(
        kernel,
        out_shape=jax.ShapeDtypeStruct((64, 2048), BF16),
        in_specs=[vmem] * 4 + [smem] * 3 + [vmem] * 3,
        out_specs=vmem,
        scratch_shapes=[
            pltpu.VMEM((8, 64, 2048), BF16),
            pltpu.VMEM((8, 16, 128), F32),
            pltpu.VMEM((8, 16, 128), F32),
            pltpu.VMEM((512, 2048), BF16),
            pltpu.VMEM((512, 2048), BF16),
            pltpu.VMEM((8, 2048, 256), BF16),
            pltpu.VMEM((8, 2048, 128), BF16),
            pltpu.VMEM((2048, 256), BF16),
            pltpu.VMEM((2048, 128), BF16),
            pltpu.VMEM((512, 1024), F32),
            pltpu.VMEM((256, 1024), BF16),
            pltpu.VMEM((2, 512, 1024), BF16),
            pltpu.VMEM((2, 512, 1024), BF16),
            pltpu.VMEM((2, 4, 128, 128), BF16),
            pltpu.VMEM((2, 4, 128, 128), BF16),
            pltpu.VMEM((2, 4, 128, 1024), F32),
            pltpu.VMEM((2, 2, 4, 64, 1024), BF16),
            pltpu.VMEM((2, 2, 4, 64, 1024), BF16),
            dma((CHUNKS, 9)),
            dma((CHUNKS, 9)),
            dma((2, 4)),
            dma((2, 4)),
            dma((2, 4)),
            dma((2, 4)),
            dma((8,)),
            dma((8,)),
            dma((4, 8)),
            dma((4, 8)),
            dma((2, 4, 8)),
            dma((2, 4, 8)),
            dma((2, 2, 4)),
            dma((2, 2, 4)),
        ],
        compiler_params=pltpu.CompilerParams(
            collective_id=0, has_side_effects=True, vmem_limit_bytes=56 * 2**20
        ),
        name="experts",
    )(
        tokens,
        route_gates.T,
        expert_ids.T,
        slot_index.T,
        gate_scale.reshape(16),
        up_scale.reshape(16),
        down_scale.reshape(16),
        gate_quant[0],
        up_quant[0],
        down_quant[0],
    )


def solution(mesh):
    return jax.shard_map(
        local,
        mesh=mesh,
        in_specs=(
            P(("stream", "expert"), None),
            P(("stream", "expert"), None),
            P(("stream", "expert"), None),
            P(("stream", "expert"), None),
            P("expert", None, "stream"),
            P("expert", None, "stream"),
            P("expert", None, "stream"),
            P("expert", None, "stream"),
            P("expert", None, "stream"),
            P("expert", None, "stream"),
        ),
        out_specs=P(("stream", "expert"), None),
        check_vma=False,
    )
```
